32 devices in a mesh: group: 2 (over x), patch: 8 (over z, y), head: 2 (over core).
Axes of the slice: x: 2, y: 2, z: 4, core: 2. Of those that a mesh axis runs over, the one named last changes fastest.
Arguments:
- q_raw: bfloat16 [1536, 1536], P(('group', 'patch', 'head')), parts along dimension 0, may hold values from -2.5 to 2.5
- k_raw: bfloat16 [1536, 1536], P(('group', 'patch', 'head')), parts along dimension 0, may hold values from -2.5 to 2.5
- v_raw: bfloat16 [1536, 1536], P(('group', 'patch', 'head')), parts along dimension 0, may hold values from -6 to 6
- q_gain: float32 [128], replicated, may hold values from 1.5 to 6
- k_gain: float32 [128], replicated, may hold values from 1.5 to 6
- base_kv: bfloat16 [2, 1536, 1536], P(None, 'group', 'head'), parts along dimension 1, may hold values from -6 to 6
- exponents: int32 [2, 12, 16], P(None, None, 'group'), parts along dimension 2, may hold values from -3 to 0
- order: int32 [1536], P('group'), parts along dimension 0, may hold values from 0 to 767, each once
Outputs:
- attn_out: bfloat16 [1536, 1536], P(('group', 'patch', 'head')), parts along dimension 0
The draws below stay inside these ranges and needn't reach their ends.
There are 2 independent parts, one for each index of `group`. The reference program is written for one: setup_inputs(seed, part) draws one part's arguments, and reference() takes and returns one part's arrays. A program takes and returns all parts, laid end to end along the dimension named above; an argument that names none is the same for every part. Nothing has to cross between parts.
Inputs may be any that keep to these rules, and one draw needn't show every extreme that they name: order is a permutation of the 768 positions.
All inputs are finite; a program needn't handle non-finite values.
Results may differ from the reference program's by a relative error of at most 0.003.
The reference program's roundings to bfloat16 on the way count: a program that leaves them out, or rounds other values in their place, can miss the bound.
Values may be sent and summed in bfloat16 or wider, within the bound.
A program may use at most 128 MiB of HBM per device.

```python
import jax
import jax.numpy as jnp
from jax import lax

HEADS = 12
HD = 128
FH = 16
FW = 16
PATCH_TOK = 96
TOKENS = 768
PATCHES = 8


def shared_rows(key):
    return jax.random.uniform(jax.random.fold_in(key, 91), (TOKENS, HEADS * HD), jnp.float32, -1.7, 1.7)


def draw_q_raw(key, part):
    shared = shared_rows(key)
    key = jax.random.fold_in(key, 1)
    values = jax.random.truncated_normal(key, -2.5, 2.5, shared.shape, jnp.float32)
    return values.astype(jnp.bfloat16)


def draw_k_raw(key, part):
    shared = shared_rows(key)
    key = jax.random.fold_in(key, 2)
    values = jax.random.truncated_normal(key, -2.5, 2.5, shared.shape, jnp.float32)
    return values.astype(jnp.bfloat16)


def draw_q_gain(key, part):
    key = jax.random.fold_in(key, 5)
    values = jax.random.uniform(key, (HD,), jnp.float32, 1.5, 3.0)
    return values


def draw_k_gain(key, part):
    key = jax.random.fold_in(key, 6)
    values = jax.random.uniform(key, (HD,), jnp.float32, 1.5, 3.0)
    return values


def touch_ends(entries, rng, smallest, largest):
    extent = entries.shape
    place = [jax.random.randint(jax.random.fold_in(rng, axis), (), 0, extent[axis]) for axis in range(len(extent))]
    entries = entries.at[tuple(place)].set(smallest)
    longest = extent.index(max(extent))
    place[longest] = (place[longest] + 1) % extent[longest]
    return entries.at[tuple(place)].set(largest)


def block_levels(rng, shape, shards, least, top_value):
    loudness, own = 1.0, jax.random.fold_in(rng, 6)
    for dim, blocks in shards:
        draws = jnp.exp(jax.random.uniform(jax.random.fold_in(own, dim), (blocks,), jnp.float32, least / len(shards), top_value / len(shards)))
        loudness = loudness * jnp.repeat(draws, shape[dim] // blocks).reshape([-1 if axis == dim else 1 for axis in range(len(shape))])
    return loudness


def noise(rng, dims, width, most, split=(), kind=jnp.bfloat16):
    array = width * jax.random.normal(rng, dims, jnp.float32)
    if split:
        array = array * block_levels(rng, dims, split, -0.22, 0.18)
    return jnp.clip(array, -most, most).astype(kind)


def setup_inputs(seed: int = 0, part: int = 0) -> dict:
    key_list = jax.random.split(jax.random.key(seed), 9)
    own_keys = jax.random.split(jax.random.fold_in(key_list[8], part), 9)
    q_raw = draw_q_raw(jax.random.fold_in(jax.random.fold_in(key_list[8], part), 71), part)
    k_raw = draw_k_raw(jax.random.fold_in(jax.random.fold_in(key_list[8], part), 71), part)
    v_raw = noise(own_keys[2], (TOKENS, HEADS * HD), 1.0, 6.0, ((0, 16),))
    q_gain = draw_q_gain(jax.random.fold_in(key_list[8], 71), part)
    k_gain = draw_k_gain(jax.random.fold_in(key_list[8], 71), part)
    base_kv = noise(own_keys[5], (2, TOKENS, HEADS * HD), 1.5, 6.0, ((2, 2),))
    exponents = touch_ends(jax.random.randint(own_keys[6], (2, HEADS, PATCHES), -3, 1), jax.random.fold_in(own_keys[6], 1), -3, 0).astype(jnp.int32)
    order = jax.random.permutation(own_keys[7], TOKENS).astype(jnp.int32)
    return {"q_raw": q_raw, "k_raw": k_raw, "v_raw": v_raw, "q_gain": q_gain, "k_gain": k_gain, "base_kv": base_kv, "exponents": exponents, "order": order}


clip_bound = 8.0
rope_theta = 256.0

def rope_angles(positions, head_size):
    frame_pos = (positions // (FH * FW)).astype(jnp.float32)
    row_pos = (positions // FW % FH).astype(jnp.float32)
    col_pos = (positions % FW).astype(jnp.float32)
    pieces = []
    for coordinate, band_width in ((frame_pos, head_size // 8), (row_pos, 7 * head_size // 16), (col_pos, 7 * head_size // 16)):
        inverse = rope_theta ** (-jnp.arange(0, band_width, 2, dtype=jnp.float32) / band_width)
        pieces.append(coordinate[:, None] * inverse[None, :])
    return jnp.concatenate(pieces, axis=1)

def normed_rotated(raw, gain, positions, head_size):
    count = raw.shape[0]
    values_f = raw.astype(jnp.float32).reshape(count, -1, head_size)
    values_f = values_f * lax.rsqrt(lax.optimization_barrier(jnp.mean(values_f * values_f, axis=-1, keepdims=True)) + 1e-06) * gain
    angles = rope_angles(positions, head_size)[:, None, :]
    paired = values_f.reshape(count, values_f.shape[1], head_size // 2, 2)
    first = paired[..., 0]
    second = paired[..., 1]
    cosine = jnp.cos(angles)
    sine = jnp.sin(angles)
    rotated = jnp.stack([first * cosine - second * sine, first * sine + second * cosine], axis=-1)
    return rotated.reshape(count, -1).astype(jnp.bfloat16)

def reference(q_raw, k_raw, v_raw, q_gain, k_gain, base_kv, exponents, order):
    positions = order
    queries = normed_rotated(q_raw, q_gain, positions, HD)
    fresh_keys = normed_rotated(k_raw, k_gain, positions, HD)
    fresh = jnp.stack([fresh_keys, v_raw]).astype(jnp.float32).reshape(2, TOKENS, HEADS, HD)
    base_rows = jnp.take(base_kv, positions, axis=1).astype(jnp.float32).reshape(2, TOKENS, HEADS, HD)
    patch_ids = jnp.arange(TOKENS, dtype=jnp.int32) // PATCH_TOK
    row_exp = jnp.take(exponents.astype(jnp.float32), patch_ids, axis=2).transpose(0, 2, 1)[..., None]
    coded = jnp.clip((fresh - base_rows) * jnp.exp2(-row_exp), -clip_bound, clip_bound).astype(jnp.bfloat16)
    rebuilt = (base_rows + coded.astype(jnp.float32) * jnp.exp2(row_exp)).astype(jnp.bfloat16)
    key_heads = rebuilt[0].transpose(1, 0, 2)
    value_heads = rebuilt[1].transpose(1, 0, 2)
    query_heads = queries.reshape(TOKENS, HEADS, HD).transpose(1, 0, 2)

    def one_head(triple_in):
        query_one, key_one, value_one = triple_in
        scores = jnp.dot(query_one, key_one.T, preferred_element_type=jnp.float32) * HD ** (-0.5)
        row_max = lax.optimization_barrier(jnp.max(scores, axis=-1, keepdims=True))
        weights = jnp.exp(scores - row_max)
        row_total = lax.optimization_barrier(jnp.sum(weights, axis=-1, keepdims=True))
        result = jnp.dot(weights.astype(jnp.bfloat16), value_one, preferred_element_type=jnp.float32) / row_total
        return result.astype(jnp.bfloat16)
    outputs = lax.map(one_head, (query_heads, key_heads, value_heads))
    return outputs.transpose(1, 0, 2).reshape(TOKENS, HEADS * HD)
```

```python
import functools

import jax
import jax.numpy as jnp
from jax import lax
from jax.experimental import pallas as pl
from jax.experimental.pallas import tpu as pltpu
from jax.sharding import PartitionSpec as P

FH = 16
FW = 16
LANES = 128

clip_bound = 8.0
rope_theta = 256.0


def kernel(
    sizes, q_ref, k_ref, v_ref, qg_ref, kg_ref, exp_ref, order_ref, base_ref, out_ref,
    send_buf, recv_buf, base_buf, pos_buf, slot_base, cos_buf, sin_buf,
    q_buf, key_buf, val_buf, o_send, o_recv,
    base_sem, send_sem, recv_sem, osend_sem, orecv_sem,
):
    n, cores, local_heads, rows = sizes
    blocks = n * cores
    heads = local_heads * cores
    hd = LANES
    tokens = blocks * rows
    patch_rows = cores * rows
    first_worker = (n - local_heads) // 2
    patch = lax.axis_index("patch")
    core = lax.axis_index("head")
    me = patch * cores + core
    local_head = patch - first_worker
    is_worker = jnp.logical_and(local_head >= 0, local_head < local_heads)
    my_head = core * local_heads + local_head

    def block_device(block):
        return {"patch": block // cores, "head": block % cores}

    def head_device(head):
        return {"patch": first_worker + head % local_heads, "head": head // local_heads}

    def in_copy(head, block):
        return pltpu.make_async_remote_copy(
            src_ref=send_buf.at[head],
            dst_ref=recv_buf.at[block],
            send_sem=send_sem.at[head],
            recv_sem=recv_sem.at[block],
            device_id=head_device(head),
            device_id_type=pl.DeviceIdType.MESH,
        )

    def out_copy(block, head):
        return pltpu.make_async_remote_copy(
            src_ref=o_send.at[block],
            dst_ref=o_recv.at[head],
            send_sem=osend_sem.at[block],
            recv_sem=orecv_sem.at[head],
            device_id=block_device(block),
            device_id_type=pl.DeviceIdType.MESH,
        )

    def base_copy(which):
        column = pl.multiple_of(local_head * hd, hd)
        return pltpu.make_async_copy(
            base_ref.at[which, :, pl.ds(column, hd)],
            base_buf.at[:, pl.ds(which * hd, hd)],
            base_sem.at[which],
        )

    barrier = pltpu.get_barrier_semaphore()

    @pl.loop(1, blocks)
    def _(step):
        pl.semaphore_signal(
            barrier, inc=1, device_id=block_device((me + step) % blocks),
            device_id_type=pl.DeviceIdType.MESH,
        )

    @pl.when(is_worker)
    def _():
        base_copy(0).start()
        base_copy(1).start()

    for head in range(heads):
        column = slice(head * hd, (head + 1) * hd)
        send_buf[head, 0] = k_ref[:, column]
        send_buf[head, 1] = v_ref[:, column]
        send_buf[head, 2] = q_ref[:, column]

    @pl.when(is_worker)
    def _():
        recv_buf[me] = send_buf[my_head]

    pl.semaphore_wait(barrier, blocks - 1)

    def is_mine(head):
        return jnp.logical_and(is_worker, head == my_head)

    @pl.loop(0, heads)
    def _(step):
        head = (me + step) % heads

        @pl.when(jnp.logical_not(is_mine(head)))
        def _():
            in_copy(head, me).start()

    @pl.when(is_worker)
    def _():
        lane = lax.broadcasted_iota(jnp.int32, (1, hd), 1)
        pair = lane // 2
        even = lane % 2 == 0
        band = hd // 16
        wide = (hd // 2 - band) // 2
        in_frame = pair < band
        in_row = pair < band + wide
        start = jnp.where(in_frame, 0, jnp.where(in_row, band, band + wide))
        width = jnp.where(in_frame, float(band), float(wide))
        ratio = (pair - start).astype(jnp.float32) / width
        inverse = jnp.exp(ratio * (-5.545177444479562))
        for j in range(tokens // LANES):
            piece = order_ref[:, j * LANES : (j + 1) * LANES]
            pos_buf[j * LANES : (j + 1) * LANES, :] = jnp.transpose(
                jnp.broadcast_to(piece, (LANES, LANES))
            )
        base_copy(0).wait()
        base_copy(1).wait()

        @pl.loop(0, n)
        def _(b):
            where = pl.ds(pl.multiple_of(b * patch_rows, 16), patch_rows)
            pos = pos_buf[where, :]
            one_hot = jnp.concatenate(
                [
                    jnp.where(pos == lane + j * LANES, 1.0, 0.0).astype(jnp.bfloat16)
                    for j in range(tokens // LANES)
                ],
                axis=1,
            )
            slot_base[where, :] = jnp.dot(
                one_hot, base_buf[...], preferred_element_type=jnp.float32
            )
            coordinate = jnp.where(
                in_frame,
                pos // (FH * FW),
                jnp.where(in_row, pos // FW % FH, pos % FW),
            ).astype(jnp.float32)
            angles = coordinate * inverse
            sine = jnp.sin(angles)
            cos_buf[where, :] = jnp.cos(angles)
            sin_buf[where, :] = jnp.where(even, -sine, sine)

        def normed_rotated(raw, gain, cosine, sine):
            mean = jnp.sum(raw * raw, axis=-1, keepdims=True) * (1.0 / hd)
            x = raw * lax.rsqrt(mean + 1e-06) * gain
            swapped = jnp.where(even, pltpu.roll(x, hd - 1, 1), pltpu.roll(x, 1, 1))
            return (x * cosine + swapped * sine).astype(jnp.bfloat16)

        def rebuilt(fresh, base, exponent):
            power = jnp.full((1, hd), exponent, jnp.int32).astype(jnp.float32)
            coded = jnp.clip((fresh - base) * jnp.exp2(-power), -clip_bound, clip_bound)
            coded = coded.astype(jnp.bfloat16).astype(jnp.float32)
            return (base + coded * jnp.exp2(power)).astype(jnp.bfloat16)

        @pl.loop(0, n)
        def _(b):
            for c in range(cores):
                block = b * cores + c

                @pl.when(block != me)
                def _():
                    in_copy(my_head, block).wait_recv()

                where = pl.ds(pl.multiple_of(block * rows, 16), rows)
                cosine = cos_buf[where, :]
                sine = sin_buf[where, :]
                k_raw = recv_buf[block, 0].astype(jnp.float32)
                v_raw = recv_buf[block, 1].astype(jnp.float32)
                q_raw = recv_buf[block, 2].astype(jnp.float32)
                q_buf[where, :] = normed_rotated(q_raw, qg_ref[...], cosine, sine)
                fresh = normed_rotated(k_raw, kg_ref[...], cosine, sine).astype(jnp.float32)
                key_buf[where, :] = rebuilt(
                    fresh, slot_base[where, :hd], exp_ref[0, my_head, b]
                )
                val_buf[where, :] = rebuilt(
                    v_raw, slot_base[where, hd:], exp_ref[1, my_head, b]
                )

        tile = 2 * patch_rows
        per_tile = tile // rows
        score_scale = hd ** (-0.5)

        @pl.loop(0, tokens // tile)
        def _(t):
            where = pl.ds(pl.multiple_of(t * tile, 16), tile)
            scores = lax.dot_general(
                q_buf[where, :], key_buf[...], (((1,), (1,)), ((), ())),
                preferred_element_type=jnp.float32,
            ) * score_scale
            weights = jnp.exp(scores - jnp.max(scores, axis=-1, keepdims=True))
            total = jnp.sum(weights, axis=-1, keepdims=True)
            accum = jnp.dot(
                weights.astype(jnp.bfloat16), val_buf[...], preferred_element_type=jnp.float32
            )
            result = (accum / total).astype(jnp.bfloat16)
            for i in range(per_tile):
                block = t * per_tile + i
                o_send[block] = result[i * rows : (i + 1) * rows]

                @pl.when(block != me)
                def _():
                    out_copy(block, my_head).start()

        o_recv[my_head] = o_send[me]

    for head in range(heads):
        @pl.when(jnp.logical_not(is_mine(head)))
        def _():
            out_copy(me, head).wait_recv()

        out_ref[:, head * hd : (head + 1) * hd] = o_recv[head]

    @pl.loop(0, heads)
    def _(head):
        @pl.when(jnp.logical_not(is_mine(head)))
        def _():
            in_copy(head, me).wait_send()

    @pl.when(is_worker)
    def _():
        @pl.loop(0, blocks)
        def _(block):
            @pl.when(block != me)
            def _():
                out_copy(block, my_head).wait_send()


def per_device(q_raw, k_raw, v_raw, q_gain, k_gain, base_kv, exponents, order):
    rows = q_raw.shape[0]
    hd = q_gain.shape[0]
    heads = q_raw.shape[1] // hd
    n = lax.axis_size("patch")
    cores = lax.axis_size("head")
    blocks = n * cores
    tokens = blocks * rows
    vmem = pl.BlockSpec(memory_space=pltpu.VMEM)
    return pl.pallas_call(
        functools.partial(kernel, (n, cores, heads // cores, rows)),
        out_shape=jax.ShapeDtypeStruct(q_raw.shape, jnp.bfloat16),
        in_specs=[vmem] * 5
        + [pl.BlockSpec(memory_space=pltpu.SMEM), vmem, pl.BlockSpec(memory_space=pl.ANY)],
        out_specs=vmem,
        scratch_shapes=[
            pltpu.VMEM((heads, 3, rows, hd), jnp.bfloat16),
            pltpu.VMEM((blocks, 3, rows, hd), jnp.bfloat16),
            pltpu.VMEM((tokens, 2 * hd), jnp.bfloat16),
            pltpu.VMEM((tokens, hd), jnp.int32),
            pltpu.VMEM((tokens, 2 * hd), jnp.float32),
            pltpu.VMEM((tokens, hd), jnp.float32),
            pltpu.VMEM((tokens, hd), jnp.float32),
            pltpu.VMEM((tokens, hd), jnp.bfloat16),
            pltpu.VMEM((tokens, hd), jnp.bfloat16),
            pltpu.VMEM((tokens, hd), jnp.bfloat16),
            pltpu.VMEM((blocks, rows, hd), jnp.bfloat16),
            pltpu.VMEM((heads, rows, hd), jnp.bfloat16),
            pltpu.SemaphoreType.DMA((2,)),
            pltpu.SemaphoreType.DMA((heads,)),
            pltpu.SemaphoreType.DMA((blocks,)),
            pltpu.SemaphoreType.DMA((blocks,)),
            pltpu.SemaphoreType.DMA((heads,)),
        ],
        compiler_params=pltpu.CompilerParams(
            collective_id=0, has_side_effects=True, vmem_limit_bytes=40 * 2**20
        ),
    )(
        q_raw, k_raw, v_raw, q_gain.reshape(1, hd), k_gain.reshape(1, hd), exponents,
        order.reshape(1, tokens), base_kv,
    )


def solution(mesh):
    in_specs = (
        P(("group", "patch", "head"), None),
        P(("group", "patch", "head"), None),
        P(("group", "patch", "head"), None),
        P(),
        P(),
        P(None, "group", "head"),
        P(None, None, "group"),
        P("group"),
    )
    out_specs = P(("group", "patch", "head"), None)
    return jax.shard_map(
        per_device, mesh=mesh, in_specs=in_specs, out_specs=out_specs, check_vma=False
    )
```

```python
import functools

import jax
import jax.numpy as jnp
from jax import lax
from jax.experimental import pallas as pl
from jax.experimental.pallas import tpu as pltpu
from jax.sharding import PartitionSpec as P

FH = 16
FW = 16
LANES = 128

clip_bound = 8.0
rope_theta = 256.0


def kernel(
    sizes, q_ref, k_ref, v_ref, qg_ref, kg_ref, exp_ref, order_ref, base_ref, out_ref,
    raw_buf, gain_buf, exp_buf, order_buf, scale_buf, send_buf, recv_buf, base_buf, pos_buf, slot_base, cos_buf, sin_buf,
    q_buf, key_buf, val_buf, o_send, o_recv,
    in_sem, small_sem, base_sem, send_sem, recv_sem, osend_sem, orecv_sem,
):
    n, cores, local_heads, rows = sizes
    blocks = n * cores
    heads = local_heads * cores
    hd = LANES
    tokens = blocks * rows
    patch_rows = cores * rows
    first_worker = (n - local_heads) // 2
    patch = lax.axis_index("patch")
    core = lax.axis_index("head")
    me = patch * cores + core
    local_head = patch - first_worker
    is_worker = jnp.logical_and(local_head >= 0, local_head < local_heads)
    my_head = core * local_heads + local_head

    def block_device(block):
        return {"patch": block // cores, "head": block % cores}

    def head_device(head):
        return {"patch": first_worker + head % local_heads, "head": head // local_heads}

    def in_copy(head, block):
        return pltpu.make_async_remote_copy(
            src_ref=send_buf.at[head],
            dst_ref=recv_buf.at[block],
            send_sem=send_sem.at[head],
            recv_sem=recv_sem.at[block],
            device_id=head_device(head),
            device_id_type=pl.DeviceIdType.MESH,
        )

    def out_copy(block, head):
        return pltpu.make_async_remote_copy(
            src_ref=o_send.at[block],
            dst_ref=o_recv.at[head],
            send_sem=osend_sem.at[block],
            recv_sem=orecv_sem.at[head],
            device_id=block_device(block),
            device_id_type=pl.DeviceIdType.MESH,
        )

    def base_copy(which):
        column = pl.multiple_of(local_head * hd, hd)
        return pltpu.make_async_copy(
            base_ref.at[which, :, pl.ds(column, hd)],
            base_buf.at[:, pl.ds(which * hd, hd)],
            base_sem.at[which],
        )

    in_copies = [
        pltpu.make_async_copy(ref, raw_buf.at[i], in_sem.at[i])
        for i, ref in enumerate((k_ref, v_ref, q_ref))
    ]
    small_copies = [
        pltpu.make_async_copy(src, dst, small_sem.at[i])
        for i, (src, dst) in enumerate(
            (
                (order_ref, order_buf),
                (exp_ref, exp_buf),
                (qg_ref, gain_buf.at[0]),
                (kg_ref, gain_buf.at[1]),
            )
        )
    ]
    for copy in in_copies:
        copy.start()

    barrier = pltpu.get_barrier_semaphore()

    @pl.loop(1, blocks)
    def _(step):
        pl.semaphore_signal(
            barrier, inc=1, device_id=block_device((me + step) % blocks),
            device_id_type=pl.DeviceIdType.MESH,
        )

    @pl.when(is_worker)
    def _():
        for copy in small_copies:
            copy.start()
        base_copy(0).start()
        base_copy(1).start()

    for i, copy in enumerate(in_copies):
        copy.wait()
        for head in range(heads):
            send_buf[head, i] = raw_buf[i, :, head * hd : (head + 1) * hd]

    @pl.when(is_worker)
    def _():
        recv_buf[me] = send_buf[my_head]

    pl.semaphore_wait(barrier, blocks - 1)

    def is_mine(head):
        return jnp.logical_and(is_worker, head == my_head)

    lower = patch < n // 2
    half_heads = local_heads // 2
    for step in range(local_heads):
        if local_heads % 2 == 0:
            across = (step < half_heads) == lower
            target = (patch + step) % half_heads + jnp.where(across, half_heads, 0)
        else:
            target = (patch + step) % local_heads
        for c in range(cores):
            head = ((core + c) % cores) * local_heads + target

            @pl.when(jnp.logical_not(is_mine(head)))
            def _():
                in_copy(head, me).start()

    @pl.when(is_worker)
    def _():
        lane = lax.broadcasted_iota(jnp.int32, (1, hd), 1)
        pair = lane // 2
        even = lane % 2 == 0
        band = hd // 16
        wide = (hd // 2 - band) // 2
        in_frame = pair < band
        in_row = pair < band + wide
        start = jnp.where(in_frame, 0, jnp.where(in_row, band, band + wide))
        width = jnp.where(in_frame, float(band), float(wide))
        ratio = (pair - start).astype(jnp.float32) / width
        inverse = jnp.exp(ratio * (-5.545177444479562))
        for copy in small_copies:
            copy.wait()
        for which in range(2):
            mine = lax.broadcasted_iota(jnp.int32, (n, heads), 1) == my_head
            power = jnp.sum(
                jnp.where(mine, exp_buf[which].astype(jnp.float32), 0.0), axis=-1, keepdims=True
            )
            power = jnp.broadcast_to(power, (n, hd))
            scale_buf[which, 0] = jnp.exp2(-power)
            scale_buf[which, 1] = jnp.exp2(power)
        for j in range(tokens // LANES):
            piece = order_buf[j * LANES : (j + 1) * LANES].reshape(1, LANES)
            pos_buf[j * LANES : (j + 1) * LANES, :] = jnp.transpose(
                jnp.broadcast_to(piece, (LANES, LANES))
            )
        base_copy(0).wait()
        base_copy(1).wait()

        @pl.loop(0, n)
        def _(b):
            where = pl.ds(pl.multiple_of(b * patch_rows, 16), patch_rows)
            pos = pos_buf[where, :]
            one_hot = jnp.concatenate(
                [
                    jnp.where(pos == lane + j * LANES, 1.0, 0.0).astype(jnp.bfloat16)
                    for j in range(tokens // LANES)
                ],
                axis=1,
            )
            slot_base[where, :] = jnp.dot(
                one_hot, base_buf[...], preferred_element_type=jnp.float32
            )
            coordinate = jnp.where(
                in_frame,
                pos // (FH * FW),
                jnp.where(in_row, pos // FW % FH, pos % FW),
            ).astype(jnp.float32)
            angles = coordinate * inverse
            sine = jnp.sin(angles)
            cos_buf[where, :] = jnp.cos(angles)
            sin_buf[where, :] = jnp.where(even, -sine, sine)

        def normed_rotated(raw, gain, cosine, sine):
            mean = jnp.sum(raw * raw, axis=-1, keepdims=True) * (1.0 / hd)
            x = raw * lax.rsqrt(mean + 1e-06) * gain
            swapped = jnp.where(even, pltpu.roll(x, hd - 1, 1), pltpu.roll(x, 1, 1))
            return (x * cosine + swapped * sine).astype(jnp.bfloat16)

        def rebuilt(fresh, base, which, b):
            down = scale_buf[which, 0, pl.ds(b, 1), :]
            up = scale_buf[which, 1, pl.ds(b, 1), :]
            coded = jnp.clip((fresh - base) * down, -clip_bound, clip_bound)
            coded = coded.astype(jnp.bfloat16).astype(jnp.float32)
            return (base + coded * up).astype(jnp.bfloat16)

        @pl.loop(0, n)
        def _(i):
            b = (i + jnp.where(lower, 0, n // 2)) % n
            for c in range(cores):
                block = b * cores + c

                @pl.when(block != me)
                def _():
                    in_copy(my_head, block).wait_recv()

                where = pl.ds(pl.multiple_of(block * rows, 16), rows)
                cosine = cos_buf[where, :]
                sine = sin_buf[where, :]
                k_raw = recv_buf[block, 0].astype(jnp.float32)
                v_raw = recv_buf[block, 1].astype(jnp.float32)
                q_raw = recv_buf[block, 2].astype(jnp.float32)
                q_buf[where, :] = normed_rotated(q_raw, gain_buf[0], cosine, sine)
                fresh = normed_rotated(k_raw, gain_buf[1], cosine, sine).astype(jnp.float32)
                key_buf[where, :] = rebuilt(
                    fresh, slot_base[where, :hd], 0, b
                )
                val_buf[where, :] = rebuilt(
                    v_raw, slot_base[where, hd:], 1, b
                )

        tile = 2 * patch_rows
        per_tile = tile // rows
        score_scale = hd ** (-0.5)

        tiles = tokens // tile

        @pl.loop(0, tiles)
        def _(step):
            t = jnp.where(lower, tiles - 1 - step, step)
            where = pl.ds(pl.multiple_of(t * tile, 16), tile)
            scores = lax.dot_general(
                q_buf[where, :], key_buf[...], (((1,), (1,)), ((), ())),
                preferred_element_type=jnp.float32,
            ) * score_scale
            weights = jnp.exp(scores - jnp.max(scores, axis=-1, keepdims=True))
            total = jnp.sum(weights, axis=-1, keepdims=True)
            accum = jnp.dot(
                weights.astype(jnp.bfloat16), val_buf[...], preferred_element_type=jnp.float32
            )
            result = (accum / total).astype(jnp.bfloat16)
            for i in range(per_tile):
                block = t * per_tile + i
                o_send[block] = result[i * rows : (i + 1) * rows]

                @pl.when(block != me)
                def _():
                    out_copy(block, my_head).start()

        o_recv[my_head] = o_send[me]

    for head in range(heads):
        @pl.when(jnp.logical_not(is_mine(head)))
        def _():
            out_copy(me, head).wait_recv()

        out_ref[:, head * hd : (head + 1) * hd] = o_recv[head]

    @pl.loop(0, heads)
    def _(head):
        @pl.when(jnp.logical_not(is_mine(head)))
        def _():
            in_copy(head, me).wait_send()

    @pl.when(is_worker)
    def _():
        @pl.loop(0, blocks)
        def _(block):
            @pl.when(block != me)
            def _():
                out_copy(block, my_head).wait_send()


def per_device(q_raw, k_raw, v_raw, q_gain, k_gain, base_kv, exponents, order):
    rows = q_raw.shape[0]
    hd = q_gain.shape[0]
    heads = q_raw.shape[1] // hd
    n = lax.axis_size("patch")
    cores = lax.axis_size("head")
    blocks = n * cores
    tokens = blocks * rows
    return pl.pallas_call(
        functools.partial(kernel, (n, cores, heads // cores, rows)),
        out_shape=jax.ShapeDtypeStruct(q_raw.shape, jnp.bfloat16),
        in_specs=[pl.BlockSpec(memory_space=pltpu.HBM)] * 8,
        out_specs=pl.BlockSpec(memory_space=pltpu.VMEM),
        scratch_shapes=[
            pltpu.VMEM((3, rows, heads * hd), jnp.bfloat16),
            pltpu.VMEM((2, 1, hd), jnp.float32),
            pltpu.VMEM((2, n, heads), jnp.int32),
            pltpu.VMEM((tokens,), jnp.int32),
            pltpu.VMEM((2, 2, n, hd), jnp.float32),
            pltpu.VMEM((heads, 3, rows, hd), jnp.bfloat16),
            pltpu.VMEM((blocks, 3, rows, hd), jnp.bfloat16),
            pltpu.VMEM((tokens, 2 * hd), jnp.bfloat16),
            pltpu.VMEM((tokens, hd), jnp.int32),
            pltpu.VMEM((tokens, 2 * hd), jnp.float32),
            pltpu.VMEM((tokens, hd), jnp.float32),
            pltpu.VMEM((tokens, hd), jnp.float32),
            pltpu.VMEM((tokens, hd), jnp.bfloat16),
            pltpu.VMEM((tokens, hd), jnp.bfloat16),
            pltpu.VMEM((tokens, hd), jnp.bfloat16),
            pltpu.VMEM((blocks, rows, hd), jnp.bfloat16),
            pltpu.VMEM((heads, rows, hd), jnp.bfloat16),
            pltpu.SemaphoreType.DMA((3,)),
            pltpu.SemaphoreType.DMA((4,)),
            pltpu.SemaphoreType.DMA((2,)),
            pltpu.SemaphoreType.DMA((heads,)),
            pltpu.SemaphoreType.DMA((blocks,)),
            pltpu.SemaphoreType.DMA((blocks,)),
            pltpu.SemaphoreType.DMA((heads,)),
        ],
        compiler_params=pltpu.CompilerParams(
            collective_id=0, has_side_effects=True, vmem_limit_bytes=64 * 2**20 - 2**17
        ),
    )(
        q_raw, k_raw, v_raw, q_gain.reshape(1, hd), k_gain.reshape(1, hd),
        exponents.transpose(0, 2, 1), order, base_kv,
    )


def solution(mesh):
    in_specs = (
        P(("group", "patch", "head"), None),
        P(("group", "patch", "head"), None),
        P(("group", "patch", "head"), None),
        P(),
        P(),
        P(None, "group", "head"),
        P(None, None, "group"),
        P("group"),
    )
    out_specs = P(("group", "patch", "head"), None)
    return jax.shard_map(
        per_device, mesh=mesh, in_specs=in_specs, out_specs=out_specs, check_vma=False
    )
```

```python
import functools

import jax
import jax.numpy as jnp
from jax import lax
from jax.experimental import pallas as pl
from jax.experimental.pallas import tpu as pltpu
from jax.sharding import PartitionSpec as P

FH = 16
FW = 16
LANES = 128

clip_bound = 8.0
rope_theta = 256.0


def kernel(
    sizes, q_ref, k_ref, v_ref, qg_ref, kg_ref, exp_ref, order_ref, base_ref, out_ref,
    raw_buf, gain_buf, exp_buf, order_buf, scale_buf, send_buf, recv_buf, base_buf, pos_buf, slot_base, cos_buf, sin_buf,
    key_buf, val_buf, o_send, o_recv,
    in_sem, small_sem, base_sem, send_sem, recv_sem, osend_sem, orecv_sem,
):
    n, cores, local_heads, rows = sizes
    blocks = n * cores
    heads = local_heads * cores
    hd = LANES
    tokens = blocks * rows
    patch_rows = cores * rows
    first_worker = (n - local_heads) // 2
    patch = lax.axis_index("patch")
    core = lax.axis_index("head")
    me = patch * cores + core
    local_head = patch - first_worker
    is_worker = jnp.logical_and(local_head >= 0, local_head < local_heads)
    my_head = core * local_heads + local_head

    def block_device(block):
        return {"patch": block // cores, "head": block % cores}

    def head_device(head):
        return {"patch": first_worker + head % local_heads, "head": head // local_heads}

    def in_copy(part, head, block):
        which = pl.ds(0, 2) if part == 0 else pl.ds(2, 1)
        return pltpu.make_async_remote_copy(
            src_ref=send_buf.at[head, which],
            dst_ref=recv_buf.at[block, which],
            send_sem=send_sem.at[part, head],
            recv_sem=recv_sem.at[part, block],
            device_id=head_device(head),
            device_id_type=pl.DeviceIdType.MESH,
        )

    def out_copy(block, head):
        return pltpu.make_async_remote_copy(
            src_ref=o_send.at[block],
            dst_ref=o_recv.at[head],
            send_sem=osend_sem.at[block],
            recv_sem=orecv_sem.at[head],
            device_id=block_device(block),
            device_id_type=pl.DeviceIdType.MESH,
        )

    def base_copy(which):
        column = pl.multiple_of(local_head * hd, hd)
        return pltpu.make_async_copy(
            base_ref.at[which, :, pl.ds(column, hd)],
            base_buf.at[:, pl.ds(which * hd, hd)],
            base_sem.at[which],
        )

    in_copies = [
        pltpu.make_async_copy(ref, raw_buf.at[i], in_sem.at[i])
        for i, ref in enumerate((k_ref, v_ref, q_ref))
    ]
    small_copies = [
        pltpu.make_async_copy(src, dst, small_sem.at[i])
        for i, (src, dst) in enumerate(
            (
                (order_ref, order_buf),
                (exp_ref, exp_buf),
                (qg_ref, gain_buf.at[0]),
                (kg_ref, gain_buf.at[1]),
            )
        )
    ]
    for copy in in_copies:
        copy.start()

    barrier = pltpu.get_barrier_semaphore()

    @pl.loop(1, blocks)
    def _(step):
        pl.semaphore_signal(
            barrier, inc=1, device_id=block_device((me + step) % blocks),
            device_id_type=pl.DeviceIdType.MESH,
        )

    @pl.when(is_worker)
    def _():
        for copy in small_copies:
            copy.start()
        base_copy(0).start()
        base_copy(1).start()

    for i, copy in enumerate(in_copies):
        copy.wait()
        for head in range(heads):
            send_buf[head, i] = raw_buf[i, :, head * hd : (head + 1) * hd]

    @pl.when(is_worker)
    def _():
        recv_buf[me] = send_buf[my_head]

    pl.semaphore_wait(barrier, blocks - 1)

    def is_mine(head):
        return jnp.logical_and(is_worker, head == my_head)

    lower = patch < n // 2
    half_heads = local_heads // 2
    for part in range(2):
        for step in range(local_heads):
            if local_heads % 2 == 0:
                far = (step < half_heads) == (part == 0)
                target = (patch + step) % half_heads + jnp.where(lower == far, half_heads, 0)
            else:
                target = (patch + step) % local_heads
            for c in range(cores):
                head = ((core + c) % cores) * local_heads + target

                @pl.when(jnp.logical_not(is_mine(head)))
                def _():
                    in_copy(part, head, me).start()

    @pl.when(is_worker)
    def _():
        lane = lax.broadcasted_iota(jnp.int32, (1, hd), 1)
        pair = lane // 2
        even = lane % 2 == 0
        band = hd // 16
        wide = (hd // 2 - band) // 2
        in_frame = pair < band
        in_row = pair < band + wide
        start = jnp.where(in_frame, 0, jnp.where(in_row, band, band + wide))
        width = jnp.where(in_frame, float(band), float(wide))
        ratio = (pair - start).astype(jnp.float32) / width
        inverse = jnp.exp(ratio * (-5.545177444479562))
        for copy in small_copies:
            copy.wait()
        for which in range(2):
            mine = lax.broadcasted_iota(jnp.int32, (n, heads), 1) == my_head
            power = jnp.sum(
                jnp.where(mine, exp_buf[which].astype(jnp.float32), 0.0), axis=-1, keepdims=True
            )
            power = jnp.broadcast_to(power, (n, hd))
            scale_buf[which, 0] = jnp.exp2(-power)
            scale_buf[which, 1] = jnp.exp2(power)
        for j in range(tokens // LANES):
            piece = order_buf[j * LANES : (j + 1) * LANES].reshape(1, LANES)
            pos_buf[j * LANES : (j + 1) * LANES, :] = jnp.transpose(
                jnp.broadcast_to(piece, (LANES, LANES))
            )
        base_copy(0).wait()
        base_copy(1).wait()

        @pl.loop(0, n)
        def _(b):
            where = pl.ds(pl.multiple_of(b * patch_rows, 16), patch_rows)
            pos = pos_buf[where, :]
            one_hot = jnp.concatenate(
                [
                    jnp.where(pos == lane + j * LANES, 1.0, 0.0).astype(jnp.bfloat16)
                    for j in range(tokens // LANES)
                ],
                axis=1,
            )
            slot_base[where, :] = jnp.dot(
                one_hot, base_buf[...], preferred_element_type=jnp.float32
            )
            coordinate = jnp.where(
                in_frame,
                pos // (FH * FW),
                jnp.where(in_row, pos // FW % FH, pos % FW),
            ).astype(jnp.float32)
            angles = coordinate * inverse
            sine = jnp.sin(angles)
            cos_buf[where, :] = jnp.cos(angles)
            sin_buf[where, :] = jnp.where(even, -sine, sine)

        def normed_rotated(raw, gain, cosine, sine):
            mean = jnp.sum(raw * raw, axis=-1, keepdims=True) * (1.0 / hd)
            x = raw * lax.rsqrt(mean + 1e-06) * gain
            swapped = jnp.where(even, pltpu.roll(x, hd - 1, 1), pltpu.roll(x, 1, 1))
            return (x * cosine + swapped * sine).astype(jnp.bfloat16)

        def rebuilt(fresh, base, which, b):
            down = scale_buf[which, 0, pl.ds(b, 1), :]
            up = scale_buf[which, 1, pl.ds(b, 1), :]
            coded = jnp.clip((fresh - base) * down, -clip_bound, clip_bound)
            coded = coded.astype(jnp.bfloat16).astype(jnp.float32)
            return (base + coded * up).astype(jnp.bfloat16)

        @pl.loop(0, n)
        def _(i):
            b = (i + jnp.where(lower, 0, n // 2)) % n
            for c in range(cores):
                block = b * cores + c

                @pl.when(block != me)
                def _():
                    in_copy(0, my_head, block).wait_recv()

                where = pl.ds(pl.multiple_of(block * rows, 16), rows)
                cosine = cos_buf[where, :]
                sine = sin_buf[where, :]
                k_raw = recv_buf[block, 0].astype(jnp.float32)
                v_raw = recv_buf[block, 1].astype(jnp.float32)
                fresh = normed_rotated(k_raw, gain_buf[1], cosine, sine).astype(jnp.float32)
                key_buf[where, :] = rebuilt(
                    fresh, slot_base[where, :hd], 0, b
                )
                val_buf[where, :] = rebuilt(
                    v_raw, slot_base[where, hd:], 1, b
                )

        tile = 2 * patch_rows
        per_tile = tile // rows
        score_scale = hd ** (-0.5)

        tiles = tokens // tile

        @pl.loop(0, tiles)
        def _(step):
            t = (step + jnp.where(lower, 0, tiles // 2)) % tiles
            where = pl.ds(pl.multiple_of(t * tile, 16), tile)
            for i in range(per_tile):
                block = t * per_tile + i

                @pl.when(block != me)
                def _():
                    in_copy(1, my_head, block).wait_recv()

            q_raw = jnp.concatenate(
                [recv_buf[t * per_tile + i, 2] for i in range(per_tile)], axis=0
            ).astype(jnp.float32)
            queries = normed_rotated(q_raw, gain_buf[0], cos_buf[where, :], sin_buf[where, :])
            scores = lax.dot_general(
                queries, key_buf[...], (((1,), (1,)), ((), ())),
                preferred_element_type=jnp.float32,
            ) * score_scale
            weights = jnp.exp(scores - jnp.max(scores, axis=-1, keepdims=True))
            total = jnp.sum(weights, axis=-1, keepdims=True)
            accum = jnp.dot(
                weights.astype(jnp.bfloat16), val_buf[...], preferred_element_type=jnp.float32
            )
            result = (accum / total).astype(jnp.bfloat16)
            for i in range(per_tile):
                block = t * per_tile + i
                o_send[block] = result[i * rows : (i + 1) * rows]

                @pl.when(block != me)
                def _():
                    out_copy(block, my_head).start()

        o_recv[my_head] = o_send[me]

    for head in range(heads):
        @pl.when(jnp.logical_not(is_mine(head)))
        def _():
            out_copy(me, head).wait_recv()

        out_ref[:, head * hd : (head + 1) * hd] = o_recv[head]

    @pl.loop(0, heads)
    def _(head):
        @pl.when(jnp.logical_not(is_mine(head)))
        def _():
            in_copy(0, head, me).wait_send()
            in_copy(1, head, me).wait_send()

    @pl.when(is_worker)
    def _():
        @pl.loop(0, blocks)
        def _(block):
            @pl.when(block != me)
            def _():
                out_copy(block, my_head).wait_send()


def per_device(q_raw, k_raw, v_raw, q_gain, k_gain, base_kv, exponents, order):
    rows = q_raw.shape[0]
    hd = q_gain.shape[0]
    heads = q_raw.shape[1] // hd
    n = lax.axis_size("patch")
    cores = lax.axis_size("head")
    blocks = n * cores
    tokens = blocks * rows
    return pl.pallas_call(
        functools.partial(kernel, (n, cores, heads // cores, rows)),
        out_shape=jax.ShapeDtypeStruct(q_raw.shape, jnp.bfloat16),
        in_specs=[pl.BlockSpec(memory_space=pltpu.HBM)] * 8,
        out_specs=pl.BlockSpec(memory_space=pltpu.VMEM),
        scratch_shapes=[
            pltpu.VMEM((3, rows, heads * hd), jnp.bfloat16),
            pltpu.VMEM((2, 1, hd), jnp.float32),
            pltpu.VMEM((2, n, heads), jnp.int32),
            pltpu.VMEM((tokens,), jnp.int32),
            pltpu.VMEM((2, 2, n, hd), jnp.float32),
            pltpu.VMEM((heads, 3, rows, hd), jnp.bfloat16),
            pltpu.VMEM((blocks, 3, rows, hd), jnp.bfloat16),
            pltpu.VMEM((tokens, 2 * hd), jnp.bfloat16),
            pltpu.VMEM((tokens, hd), jnp.int32),
            pltpu.VMEM((tokens, 2 * hd), jnp.float32),
            pltpu.VMEM((tokens, hd), jnp.float32),
            pltpu.VMEM((tokens, hd), jnp.float32),
            pltpu.VMEM((tokens, hd), jnp.bfloat16),
            pltpu.VMEM((tokens, hd), jnp.bfloat16),
            pltpu.VMEM((blocks, rows, hd), jnp.bfloat16),
            pltpu.VMEM((heads, rows, hd), jnp.bfloat16),
            pltpu.SemaphoreType.DMA((3,)),
            pltpu.SemaphoreType.DMA((4,)),
            pltpu.SemaphoreType.DMA((2,)),
            pltpu.SemaphoreType.DMA((2, heads)),
            pltpu.SemaphoreType.DMA((2, blocks)),
            pltpu.SemaphoreType.DMA((blocks,)),
            pltpu.SemaphoreType.DMA((heads,)),
        ],
        compiler_params=pltpu.CompilerParams(
            collective_id=0, has_side_effects=True, vmem_limit_bytes=64 * 2**20 - 2**17
        ),
    )(
        q_raw, k_raw, v_raw, q_gain.reshape(1, hd), k_gain.reshape(1, hd),
        exponents.transpose(0, 2, 1), order, base_kv,
    )


def solution(mesh):
    in_specs = (
        P(("group", "patch", "head"), None),
        P(("group", "patch", "head"), None),
        P(("group", "patch", "head"), None),
        P(),
        P(),
        P(None, "group", "head"),
        P(None, None, "group"),
        P("group"),
    )
    out_specs = P(("group", "patch", "head"), None)
    return jax.shard_map(
        per_device, mesh=mesh, in_specs=in_specs, out_specs=out_specs, check_vma=False
    )
```

```python
import functools

import jax
import jax.numpy as jnp
from jax import lax
from jax.experimental import pallas as pl
from jax.experimental.pallas import tpu as pltpu
from jax.sharding import PartitionSpec as P

FH = 16
FW = 16
LANES = 128

clip_bound = 8.0
rope_theta = 256.0


def kernel(
    sizes, q_ref, k_ref, v_ref, qg_ref, kg_ref, exp_ref, order_ref, base_ref, out_ref,
    raw_buf, gain_buf, exp_buf, order_buf, scale_buf, send_buf, recv_buf, base_buf, pos_buf, slot_base, cos_buf, sin_buf,
    key_buf, val_buf, o_send, o_recv,
    in_sem, small_sem, base_sem, send_sem, recv_sem, osend_sem, orecv_sem,
):
    n, cores, local_heads, rows = sizes
    blocks = n * cores
    heads = local_heads * cores
    hd = LANES
    tokens = blocks * rows
    patch_rows = cores * rows
    first_worker = (n - local_heads) // 2
    patch = lax.axis_index("patch")
    core = lax.axis_index("head")
    me = patch * cores + core
    local_head = patch - first_worker
    is_worker = jnp.logical_and(local_head >= 0, local_head < local_heads)
    my_head = core * local_heads + local_head

    def block_device(block):
        return {"patch": block // cores, "head": block % cores}

    def head_device(head):
        return {"patch": first_worker + head % local_heads, "head": head // local_heads}

    def in_copy(part, head, block):
        which = pl.ds(0, 2) if part == 0 else pl.ds(2, 1)
        return pltpu.make_async_remote_copy(
            src_ref=send_buf.at[head, which],
            dst_ref=recv_buf.at[block, which],
            send_sem=send_sem.at[part, head],
            recv_sem=recv_sem.at[part, block],
            device_id=head_device(head),
            device_id_type=pl.DeviceIdType.MESH,
        )

    def out_copy(block, head):
        return pltpu.make_async_remote_copy(
            src_ref=o_send.at[block],
            dst_ref=o_recv.at[head],
            send_sem=osend_sem.at[block],
            recv_sem=orecv_sem.at[head],
            device_id=block_device(block),
            device_id_type=pl.DeviceIdType.MESH,
        )

    def base_copy(which):
        column = pl.multiple_of(local_head * hd, hd)
        return pltpu.make_async_copy(
            base_ref.at[which, :, pl.ds(column, hd)],
            base_buf.at[:, pl.ds(which * hd, hd)],
            base_sem.at[which],
        )

    in_copies = [
        pltpu.make_async_copy(ref, raw_buf.at[i], in_sem.at[i])
        for i, ref in enumerate((k_ref, v_ref, q_ref))
    ]
    small_copies = [
        pltpu.make_async_copy(src, dst, small_sem.at[i])
        for i, (src, dst) in enumerate(
            (
                (order_ref, order_buf),
                (exp_ref, exp_buf),
                (qg_ref, gain_buf.at[0]),
                (kg_ref, gain_buf.at[1]),
            )
        )
    ]
    for copy in in_copies:
        copy.start()

    barrier = pltpu.get_barrier_semaphore()

    @pl.loop(1, blocks)
    def _(step):
        pl.semaphore_signal(
            barrier, inc=1, device_id=block_device((me + step) % blocks),
            device_id_type=pl.DeviceIdType.MESH,
        )

    @pl.when(is_worker)
    def _():
        for copy in small_copies:
            copy.start()
        base_copy(0).start()
        base_copy(1).start()

    for i, copy in enumerate(in_copies):
        copy.wait()
        for head in range(heads):
            send_buf[head, i] = raw_buf[i, :, head * hd : (head + 1) * hd]

    @pl.when(is_worker)
    def _():
        recv_buf[me] = send_buf[my_head]

    pl.semaphore_wait(barrier, blocks - 1)

    def is_mine(head):
        return jnp.logical_and(is_worker, head == my_head)

    lower = patch < n // 2
    half_heads = local_heads // 2
    for part in range(2):
        for step in range(local_heads):
            if local_heads % 2 == 0:
                far = step < half_heads
                target = (patch + step) % half_heads + jnp.where(lower == far, half_heads, 0)
            else:
                target = (patch + step) % local_heads
            for c in range(cores):
                head = ((core + c) % cores) * local_heads + target

                @pl.when(jnp.logical_not(is_mine(head)))
                def _():
                    in_copy(part, head, me).start()

    @pl.when(is_worker)
    def _():
        lane = lax.broadcasted_iota(jnp.int32, (1, hd), 1)
        pair = lane // 2
        even = lane % 2 == 0
        band = hd // 16
        wide = (hd // 2 - band) // 2
        in_frame = pair < band
        in_row = pair < band + wide
        start = jnp.where(in_frame, 0, jnp.where(in_row, band, band + wide))
        width = jnp.where(in_frame, float(band), float(wide))
        ratio = (pair - start).astype(jnp.float32) / width
        inverse = jnp.exp(ratio * (-5.545177444479562))
        for copy in small_copies:
            copy.wait()
        for which in range(2):
            mine = lax.broadcasted_iota(jnp.int32, (n, heads), 1) == my_head
            power = jnp.sum(
                jnp.where(mine, exp_buf[which].astype(jnp.float32), 0.0), axis=-1, keepdims=True
            )
            power = jnp.broadcast_to(power, (n, hd))
            scale_buf[which, 0] = jnp.exp2(-power)
            scale_buf[which, 1] = jnp.exp2(power)
        for j in range(tokens // LANES):
            piece = order_buf[j * LANES : (j + 1) * LANES].reshape(1, LANES)
            pos_buf[j * LANES : (j + 1) * LANES, :] = jnp.transpose(
                jnp.broadcast_to(piece, (LANES, LANES))
            )
        base_copy(0).wait()
        base_copy(1).wait()

        @pl.loop(0, n)
        def _(b):
            where = pl.ds(pl.multiple_of(b * patch_rows, 16), patch_rows)
            pos = pos_buf[where, :]
            one_hot = jnp.concatenate(
                [
                    jnp.where(pos == lane + j * LANES, 1.0, 0.0).astype(jnp.bfloat16)
                    for j in range(tokens // LANES)
                ],
                axis=1,
            )
            slot_base[where, :] = jnp.dot(
                one_hot, base_buf[...], preferred_element_type=jnp.float32
            )
            coordinate = jnp.where(
                in_frame,
                pos // (FH * FW),
                jnp.where(in_row, pos // FW % FH, pos % FW),
            ).astype(jnp.float32)
            angles = coordinate * inverse
            sine = jnp.sin(angles)
            cos_buf[where, :] = jnp.cos(angles)
            sin_buf[where, :] = jnp.where(even, -sine, sine)

        def normed_rotated(raw, gain, cosine, sine):
            mean = jnp.sum(raw * raw, axis=-1, keepdims=True) * (1.0 / hd)
            x = raw * lax.rsqrt(mean + 1e-06) * gain
            swapped = jnp.where(even, pltpu.roll(x, hd - 1, 1), pltpu.roll(x, 1, 1))
            return (x * cosine + swapped * sine).astype(jnp.bfloat16)

        def rebuilt(fresh, base, which, b):
            down = scale_buf[which, 0, pl.ds(b, 1), :]
            up = scale_buf[which, 1, pl.ds(b, 1), :]
            coded = jnp.clip((fresh - base) * down, -clip_bound, clip_bound)
            coded = coded.astype(jnp.bfloat16).astype(jnp.float32)
            return (base + coded * up).astype(jnp.bfloat16)

        @pl.loop(0, n)
        def _(i):
            b = (i + jnp.where(lower, 0, n // 2)) % n
            for c in range(cores):
                block = b * cores + c

                @pl.when(block != me)
                def _():
                    in_copy(0, my_head, block).wait_recv()

                where = pl.ds(pl.multiple_of(block * rows, 16), rows)
                cosine = cos_buf[where, :]
                sine = sin_buf[where, :]
                k_raw = recv_buf[block, 0].astype(jnp.float32)
                v_raw = recv_buf[block, 1].astype(jnp.float32)
                fresh = normed_rotated(k_raw, gain_buf[1], cosine, sine).astype(jnp.float32)
                key_buf[where, :] = rebuilt(
                    fresh, slot_base[where, :hd], 0, b
                )
                val_buf[where, :] = rebuilt(
                    v_raw, slot_base[where, hd:], 1, b
                )

        tile = 2 * patch_rows
        per_tile = tile // rows
        score_scale = hd ** (-0.5)

        tiles = tokens // tile

        @pl.loop(0, tiles)
        def _(step):
            t = (step + jnp.where(lower, tiles // 2, 0)) % tiles
            where = pl.ds(pl.multiple_of(t * tile, 16), tile)
            for i in range(per_tile):
                block = t * per_tile + i

                @pl.when(block != me)
                def _():
                    in_copy(1, my_head, block).wait_recv()

            q_raw = jnp.concatenate(
                [recv_buf[t * per_tile + i, 2] for i in range(per_tile)], axis=0
            ).astype(jnp.float32)
            queries = normed_rotated(q_raw, gain_buf[0], cos_buf[where, :], sin_buf[where, :])
            scores = lax.dot_general(
                queries, key_buf[...], (((1,), (1,)), ((), ())),
                preferred_element_type=jnp.float32,
            ) * score_scale
            weights = jnp.exp(scores - jnp.max(scores, axis=-1, keepdims=True))
            total = jnp.sum(weights, axis=-1, keepdims=True)
            accum = jnp.dot(
                weights.astype(jnp.bfloat16), val_buf[...], preferred_element_type=jnp.float32
            )
            result = (accum / total).astype(jnp.bfloat16)
            for i in range(per_tile):
                block = t * per_tile + i
                o_send[block] = result[i * rows : (i + 1) * rows]

                @pl.when(block != me)
                def _():
                    out_copy(block, my_head).start()

        o_recv[my_head] = o_send[me]

    for head in range(heads):
        @pl.when(jnp.logical_not(is_mine(head)))
        def _():
            out_copy(me, head).wait_recv()

        out_ref[:, head * hd : (head + 1) * hd] = o_recv[head]

    @pl.loop(0, heads)
    def _(head):
        @pl.when(jnp.logical_not(is_mine(head)))
        def _():
            in_copy(0, head, me).wait_send()
            in_copy(1, head, me).wait_send()

    @pl.when(is_worker)
    def _():
        @pl.loop(0, blocks)
        def _(block):
            @pl.when(block != me)
            def _():
                out_copy(block, my_head).wait_send()


def per_device(q_raw, k_raw, v_raw, q_gain, k_gain, base_kv, exponents, order):
    rows = q_raw.shape[0]
    hd = q_gain.shape[0]
    heads = q_raw.shape[1] // hd
    n = lax.axis_size("patch")
    cores = lax.axis_size("head")
    blocks = n * cores
    tokens = blocks * rows
    return pl.pallas_call(
        functools.partial(kernel, (n, cores, heads // cores, rows)),
        out_shape=jax.ShapeDtypeStruct(q_raw.shape, jnp.bfloat16),
        in_specs=[pl.BlockSpec(memory_space=pltpu.HBM)] * 8,
        out_specs=pl.BlockSpec(memory_space=pltpu.VMEM),
        scratch_shapes=[
            pltpu.VMEM((3, rows, heads * hd), jnp.bfloat16),
            pltpu.VMEM((2, 1, hd), jnp.float32),
            pltpu.VMEM((2, n, heads), jnp.int32),
            pltpu.VMEM((tokens,), jnp.int32),
            pltpu.VMEM((2, 2, n, hd), jnp.float32),
            pltpu.VMEM((heads, 3, rows, hd), jnp.bfloat16),
            pltpu.VMEM((blocks, 3, rows, hd), jnp.bfloat16),
            pltpu.VMEM((tokens, 2 * hd), jnp.bfloat16),
            pltpu.VMEM((tokens, hd), jnp.int32),
            pltpu.VMEM((tokens, 2 * hd), jnp.float32),
            pltpu.VMEM((tokens, hd), jnp.float32),
            pltpu.VMEM((tokens, hd), jnp.float32),
            pltpu.VMEM((tokens, hd), jnp.bfloat16),
            pltpu.VMEM((tokens, hd), jnp.bfloat16),
            pltpu.VMEM((blocks, rows, hd), jnp.bfloat16),
            pltpu.VMEM((heads, rows, hd), jnp.bfloat16),
            pltpu.SemaphoreType.DMA((3,)),
            pltpu.SemaphoreType.DMA((4,)),
            pltpu.SemaphoreType.DMA((2,)),
            pltpu.SemaphoreType.DMA((2, heads)),
            pltpu.SemaphoreType.DMA((2, blocks)),
            pltpu.SemaphoreType.DMA((blocks,)),
            pltpu.SemaphoreType.DMA((heads,)),
        ],
        compiler_params=pltpu.CompilerParams(
            collective_id=0, has_side_effects=True, vmem_limit_bytes=64 * 2**20 - 2**17
        ),
    )(
        q_raw, k_raw, v_raw, q_gain.reshape(1, hd), k_gain.reshape(1, hd),
        exponents.transpose(0, 2, 1), order, base_kv,
    )


def solution(mesh):
    in_specs = (
        P(("group", "patch", "head"), None),
        P(("group", "patch", "head"), None),
        P(("group", "patch", "head"), None),
        P(),
        P(),
        P(None, "group", "head"),
        P(None, None, "group"),
        P("group"),
    )
    out_specs = P(("group", "patch", "head"), None)
    return jax.shard_map(
        per_device, mesh=mesh, in_specs=in_specs, out_specs=out_specs, check_vma=False
    )
```
